32 devices in a mesh: tm: 4 (over z), queue: 8 (over y, x, core).
Axes of the slice: x: 2, y: 2, z: 4, core: 2. Of those that a mesh axis runs over, the one named last changes fastest.
Arguments:
- clips: bfloat16 [8192, 512], P('tm'), may hold values from -6 to 6
- narrations: bfloat16 [8192, 512], P('tm'), may hold values from -6 to 6
- queue: bfloat16 [8192, 512], P('queue'), may hold values from -6 to 6
- loss_weights: float32 [8192], P('tm'), may hold values from 0.5 to 4
- offsets: int32 [8192, 8], P('tm'), may hold values from -4 to 4
- valid: int32 [8192, 8], P('tm'), may hold values 0 or 1
Outputs:
- grad_clips: bfloat16 [8192, 512], P(('tm', 'queue'))
- grad_narrations: bfloat16 [8192, 512], P('tm')
- grad_queue: bfloat16 [8192, 512], P('queue')
The draws below stay inside these ranges and needn't reach their ends.
All inputs are finite; a program needn't handle non-finite values. No bound on the sum of `valid` on one device may be relied on, other than what follows from the above.
Results may differ from the reference program's by a relative error of at most 0.0051.
Values may be sent and summed in bfloat16 or wider, within the bound.
A program may use at most 192 MiB of HBM per device.

```python
import math
import jax
import jax.numpy as jnp
from jax import lax

E = 512
HALO = 4
BAG = 8
CLIPS = 8192
QN = 8192


def shared_track(key):
    noise = jax.random.normal(jax.random.fold_in(key, 41), (CLIPS + 3, E), jnp.float32)
    return (noise[:-3] + noise[1:-2] + noise[2:-1] + noise[3:]) * 0.5


def sign_pattern(key):
    flips = jax.random.bernoulli(jax.random.fold_in(key, 91), 0.5, (E // 2,)).astype(jnp.float32)
    return jnp.repeat(2.0 * flips - 1.0, 2)


def embed_rows(key, track, row_count):
    noise = jax.random.normal(jax.random.fold_in(key, 1), (row_count, E), jnp.float32)
    return 0.8 * track + 0.6 * noise


def draw_clips(key, part):
    track = shared_track(key)
    pattern = sign_pattern(key)
    key = jax.random.fold_in(key, 3)
    values = embed_rows(key, track, CLIPS)
    rows = jnp.arange(CLIPS, dtype=jnp.int32)
    amplitude = 5.0 + 0.25 * (rows // 97 % 4).astype(jnp.float32)
    aligned = rows % 97 == 5
    values = jnp.where(aligned[:, None], amplitude[:, None] * pattern[None, :], values)
    return jnp.clip(values, -6.0, 6.0).astype(jnp.bfloat16)


def draw_narrations(key, part):
    track = shared_track(key)
    key = jax.random.fold_in(key, 5)
    values = embed_rows(key, track, CLIPS)
    return jnp.clip(values, -6.0, 6.0).astype(jnp.bfloat16)


def draw_queue(key, part):
    pattern = sign_pattern(key)
    key = jax.random.fold_in(key, 7)
    values = jax.random.normal(jax.random.fold_in(key, 1), (QN, E), jnp.float32)
    rows = jnp.arange(QN, dtype=jnp.int32)
    amplitude = 5.0 + 0.25 * (rows // 211 % 4).astype(jnp.float32)
    halves = jnp.clip(jax.random.normal(jax.random.fold_in(key, 6), (QN, E // 2), jnp.float32), -2.5, 2.5)
    alternate = jnp.where(jnp.arange(E, dtype=jnp.int32) % 2 == 0, 1.0, -1.0)
    wobble = 0.5 * jnp.repeat(halves, 2, axis=1) * alternate[None, :]
    first = rows % 211 == 3
    second = rows % 211 == 4
    values = jnp.where(first[:, None], amplitude[:, None] * pattern[None, :], values)
    values = jnp.where(second[:, None], (amplitude[:, None] - 0.03) * pattern[None, :] + wobble, values)
    return jnp.clip(values, -6.0, 6.0).astype(jnp.bfloat16)


def set_ends(values, key, low, largest):
    index_at = [jax.random.randint(jax.random.fold_in(key, axis), (), 0, length) for axis, length in enumerate(values.shape)]
    main_axis = values.shape.index(max(values.shape))
    neighbour = index_at[:main_axis] + [(index_at[main_axis] + 1) % values.shape[main_axis]] + index_at[main_axis + 1:]
    return values.at[tuple(index_at)].set(low).at[tuple(neighbour)].set(largest)


def levels(own_key, dims, split, low, top_value):
    gain = 1.0
    for dim, blocks in split:
        draws = jax.random.uniform(jax.random.fold_in(jax.random.fold_in(own_key, 6), dim), (blocks,), jnp.float32, low / len(split), top_value / len(split))
        gain = gain * jnp.repeat(jnp.exp(draws), dims[dim] // blocks).reshape((-1,) + (1,) * (len(dims) - 1 - dim))
    return gain


def setup_inputs(seed: int = 0) -> dict:
    key_list = jax.random.split(jax.random.key(seed), 7)
    clips = draw_clips(jax.random.fold_in(key_list[6], 71), 0)
    narrations = draw_narrations(jax.random.fold_in(key_list[6], 71), 0)
    queue = draw_queue(jax.random.fold_in(key_list[6], 71), 0)
    loss_weights = jnp.clip(jnp.exp(math.log(4.0) - 2.0794415 * jax.random.uniform(key_list[3], (CLIPS,), jnp.float32) ** levels(key_list[3], (CLIPS,), ((0, 4),), -0.2, 0.2)), 0.5, 4.0)
    offsets = set_ends(jax.random.randint(key_list[4], (CLIPS, BAG), -HALO, HALO + 1), jax.random.fold_in(key_list[4], 1), -HALO, HALO).astype(jnp.int32)
    valid = set_ends((jax.random.randint(key_list[5], (CLIPS, BAG), 0, 4) < 3).astype(jnp.int32), jax.random.fold_in(key_list[5], 1), 0, 1)
    return dict(clips=clips, narrations=narrations, queue=queue, loss_weights=loss_weights, offsets=offsets, valid=valid)


def reference(clips, narrations, queue, loss_weights, offsets, valid):
    scale = 0.75 / math.sqrt(E)
    clip_f = clips.astype(jnp.float32)
    padded = jnp.pad(narrations.astype(jnp.float32), ((HALO, HALO), (0, 0)))
    position = jnp.arange(CLIPS, dtype=jnp.int32)
    valid_f = valid.astype(jnp.float32)
    score_list = []
    count_list = []
    for delta in range(-HALO, HALO + 1):
        piece = padded[HALO + delta:HALO + delta + CLIPS]
        score_list.append(scale * lax.optimization_barrier(jnp.sum(clip_f * piece, axis=1)))
        inside = ((position + delta >= 0) & (position + delta < CLIPS)).astype(jnp.float32)
        hits = lax.optimization_barrier(jnp.sum(valid_f * (offsets == delta).astype(jnp.float32), axis=1))
        own = 1.0 if delta == 0 else 0.0
        count_list.append((own + hits) * inside)
    bag_scores = jnp.stack(score_list)
    counts = jnp.stack(count_list)
    bag_top = lax.optimization_barrier(jnp.max(jnp.where(counts > 0, bag_scores, -jnp.inf), axis=0))
    bag_sum = lax.optimization_barrier(jnp.sum(counts * jnp.exp(bag_scores - bag_top[None, :]), axis=0))
    block = math.gcd(CLIPS, 512)
    steps_count = CLIPS // block

    def step(grad_q, index):
        start = index * block
        clip_block = lax.dynamic_slice_in_dim(clips, start, block, 0)
        scores = scale * lax.dot_general(clip_block, queue, (((1,), (1,)), ((), ())), preferred_element_type=jnp.float32)
        top = lax.dynamic_slice_in_dim(bag_top, start, block, 0)
        bsum = lax.dynamic_slice_in_dim(bag_sum, start, block, 0)
        weight = lax.dynamic_slice_in_dim(loss_weights, start, block, 0)
        shift = jnp.maximum(lax.optimization_barrier(jnp.max(scores, axis=1)), top)
        expo = jnp.exp(scores - shift[:, None])
        bag_part = bsum * jnp.exp(top - shift)
        total = lax.optimization_barrier(jnp.sum(expo, axis=1)) + bag_part
        neg_coef = ((weight / total)[:, None] * expo).astype(jnp.bfloat16)
        grad_q = grad_q + lax.dot_general(neg_coef, clip_block, (((0,), (0,)), ((), ())), preferred_element_type=jnp.float32)
        return (grad_q, (jnp.dot(neg_coef, queue, preferred_element_type=jnp.float32), bag_part / total))
    grad_q, (neg_grad, share) = lax.scan(step, jnp.zeros((QN, E), jnp.float32), jnp.arange(steps_count, dtype=jnp.int32))
    neg_grad = neg_grad.reshape(CLIPS, E)
    share = share.reshape(CLIPS)
    bag_coef = (loss_weights[None, :] * counts * jnp.exp(bag_scores - bag_top[None, :]) / bag_sum[None, :] * (share[None, :] - 1.0)).astype(jnp.bfloat16)
    bag_grad = jnp.zeros((CLIPS, E), jnp.float32)
    narr_grad = jnp.zeros((CLIPS + 2 * HALO, E), jnp.float32)
    for slot, delta in enumerate(range(-HALO, HALO + 1)):
        coef = bag_coef[slot].astype(jnp.float32)[:, None]
        bag_grad = bag_grad + coef * padded[HALO + delta:HALO + delta + CLIPS]
        narr_grad = narr_grad + jnp.pad(coef * clip_f, ((HALO + delta, HALO - delta), (0, 0)))
    grad_clips = (scale * (bag_grad + neg_grad)).astype(jnp.bfloat16)
    grad_narrations = (scale * narr_grad[HALO:HALO + CLIPS]).astype(jnp.bfloat16)
    grad_queue = (scale * grad_q).astype(jnp.bfloat16)
    return (grad_clips, grad_narrations, grad_queue)
```

```python
import functools
import math

import jax
import jax.numpy as jnp
from jax import lax
from jax.experimental import pallas as pl
from jax.experimental.pallas import tpu as pltpu
from jax.sharding import PartitionSpec as P

HALO = 4
PAD = 16
BLK = 128
WIN = BLK + 2 * PAD
LAG = 2
MESH = pl.DeviceIdType.MESH
F32 = jnp.float32
BF16 = jnp.bfloat16
NT = (((1,), (1,)), ((), ()))
TN = (((0,), (0,)), ((), ()))


def dot(a, b, dims=(((1,), (0,)), ((), ()))):
    return lax.dot_general(a, b, dims, preferred_element_type=F32)


def kernel(T, Q, ZC, clips, narr_hbm, queue, weights, offsets, valid, gc_hbm, gn_hbm, gq_hbm,
           ext, scores, coef, stat, bag_s, counts, bag_c, narr_acc, edge, part, up_tx, up_rx, fin,
           grad_f, grad_b, pair_rx, chip_tx, chip_rx, bag_grad, gc_out, gn_out,
           load_sem, halo_ss, halo_rs, stat_ss, stat_rs, up_ss, up_rs, down_ss, down_rs,
           pair_ss, pair_rs, chip_ss, chip_rs, edge_ss, edge_rs, gq_sem, out_sem):
    rows, width = clips.shape
    negs = queue.shape[0]
    scale = 0.75 / math.sqrt(width)
    chips = Q // 2
    own = rows // Q
    zn = negs // ZC
    blocks = rows // BLK
    root = (T - 1) // 2
    t = lax.axis_index("tm")
    q = lax.axis_index("queue")
    chip = q // 2
    core = lax.rem(q, 2)
    has_prev = t > 0
    has_next = t < T - 1

    def remote(src, dst, ss, rs, dev):
        return pltpu.make_async_remote_copy(
            src_ref=src, dst_ref=dst, send_sem=ss, recv_sem=rs, device_id=dev, device_id_type=MESH)

    barrier = pltpu.get_barrier_semaphore()
    for k in range(1, Q):
        pl.semaphore_signal(barrier, inc=1, device_id=(t, lax.rem(q + k, Q)), device_id_type=MESH)

    @pl.when(has_prev)
    def _():
        pl.semaphore_signal(barrier, inc=1, device_id=(t - 1, q), device_id_type=MESH)

    @pl.when(has_next)
    def _():
        pl.semaphore_signal(barrier, inc=1, device_id=(t + 1, q), device_id_type=MESH)

    load = pltpu.make_async_copy(narr_hbm, ext.at[pl.ds(PAD, rows)], load_sem)
    load.start()

    SN = 256

    def score_step(k, top):
        r = pl.ds(pl.multiple_of(k * SN, SN), SN)
        s = scale * dot(queue[r, :], clips[...], NT)
        scores[r, :] = s
        return jnp.maximum(top, jnp.max(s, axis=0, keepdims=True))

    top = lax.fori_loop(0, negs // SN, score_step, jnp.full((1, rows), -jnp.inf, F32))

    load.wait()
    pl.semaphore_wait(barrier, Q - 1 + has_prev.astype(jnp.int32) + has_next.astype(jnp.int32))

    def halo_next():
        return remote(ext.at[pl.ds(rows, PAD)], ext.at[pl.ds(0, PAD)],
                      halo_ss.at[0], halo_rs.at[0], (t + 1, q))

    def halo_prev():
        return remote(ext.at[pl.ds(PAD, PAD)], ext.at[pl.ds(PAD + rows, PAD)],
                      halo_ss.at[1], halo_rs.at[1], (t - 1, q))

    @pl.when(has_next)
    def _():
        halo_next().start()

    @pl.when(has_prev)
    def _():
        halo_prev().start()

    EN = 32

    def exp_step(k, total):
        r = pl.ds(pl.multiple_of(k * EN, EN), EN)
        p = jnp.exp(scores[r, :] - top)
        scores[r, :] = p
        return total + jnp.sum(p, axis=0, keepdims=True)

    local_sum = lax.fori_loop(0, negs // EN, exp_step, jnp.zeros((1, rows), F32))
    stat[q, 0:1, :] = top
    stat[q, 1:2, :] = local_sum

    def stat_copy(k):
        peer = lax.rem(q + k, Q)
        return remote(stat.at[q], stat.at[q], stat_ss.at[k], stat_rs.at[k], (t, peer))

    def stat_arrival(k):
        source = lax.rem(q + Q - k, Q)
        return remote(stat.at[source], stat.at[source], stat_ss.at[k], stat_rs.at[k], (t, source))

    for k in range(1, Q):
        stat_copy(k).start()

    @pl.when(has_prev)
    def _():
        halo_next().wait_recv()

    @pl.when(jnp.logical_not(has_prev))
    def _():
        ext[0:PAD, :] = jnp.zeros((PAD, width), BF16)

    @pl.when(has_next)
    def _():
        halo_prev().wait_recv()

    @pl.when(jnp.logical_not(has_next))
    def _():
        ext[PAD + rows:, :] = jnp.zeros((PAD, width), BF16)

    bag_s[...] = jnp.zeros_like(bag_s)
    counts[...] = jnp.zeros_like(counts)
    delta = (lax.broadcasted_iota(jnp.int32, (WIN, BLK), 0)
             - lax.broadcasted_iota(jnp.int32, (WIN, BLK), 1) - PAD)

    def bag_step(b, _):
        i0 = pl.multiple_of(b * BLK, BLK)
        s = scale * dot(ext[pl.ds(i0, WIN), :], clips[pl.ds(i0, BLK), :], NT)
        for d in range(-HALO, HALO + 1):
            bag_s[d + HALO:d + HALO + 1, pl.ds(i0, BLK)] = jnp.sum(
                jnp.where(delta == d, s, 0.0), axis=0, keepdims=True)
        return 0

    lax.fori_loop(0, blocks, bag_step, 0)

    position = t * rows + lax.broadcasted_iota(jnp.int32, (1, rows), 1)
    used = valid[...] > 0
    for d in range(-HALO, HALO + 1):
        hits = jnp.sum(jnp.where(used & (offsets[...] == d), 1.0, 0.0), axis=0, keepdims=True)
        inside = (position + d >= 0) & (position + d < T * rows)
        counts[d + HALO:d + HALO + 1, :] = jnp.where(inside, hits + (1.0 if d == 0 else 0.0), 0.0)
    count = counts[...]
    bag_top = jnp.max(jnp.where(count > 0, bag_s[...], -jnp.inf), axis=0, keepdims=True)
    bag_e = jnp.where(count > 0, count * jnp.exp(bag_s[...] - bag_top), 0.0)
    bag_sum = jnp.sum(bag_e, axis=0, keepdims=True)

    for k in range(1, Q):
        stat_arrival(k).wait_recv()
    shift = bag_top
    for k in range(Q):
        shift = jnp.maximum(shift, stat[k, 0:1, :])
    bag_part = bag_sum * jnp.exp(bag_top - shift)
    total = bag_part
    for k in range(Q):
        total = total + stat[k, 1:2, :] * jnp.exp(stat[k, 0:1, :] - shift)
    share = bag_part / total
    w = weights[...]
    factor = w / total * jnp.exp(top - shift)
    bag_c[...] = (w * bag_e / bag_sum * (share - 1.0)).astype(BF16).astype(F32)

    left_child = has_prev & (t <= root)
    right_child = has_next & (t >= root)
    leaf = jnp.logical_not(left_child | right_child)

    def zrows(c):
        return pl.ds(pl.multiple_of(c * zn, zn), zn)

    def up_right(c):
        return remote(up_tx.at[zrows(c)], up_rx.at[0, zrows(c)], up_ss.at[c], up_rs.at[0, c], (t + 1, q))

    def up_left(c):
        return remote(up_tx.at[zrows(c)], up_rx.at[1, zrows(c)], up_ss.at[c], up_rs.at[1, c], (t - 1, q))

    def down_left(c):
        return remote(fin.at[zrows(c)], fin.at[zrows(c)], down_ss.at[0, c], down_rs.at[c], (t - 1, q))

    def down_right(c):
        return remote(fin.at[zrows(c)], fin.at[zrows(c)], down_ss.at[1, c], down_rs.at[c], (t + 1, q))

    def store_queue(c):
        return pltpu.make_async_copy(fin.at[zrows(c)], gq_hbm.at[zrows(c)], gq_sem.at[c])

    def pass_down(c):
        @pl.when(left_child)
        def _():
            down_left(c).start()

        @pl.when(right_child)
        def _():
            down_right(c).start()

        store_queue(c).start()

    def send_up(c):
        up_tx[zrows(c), :] = part[zrows(c), :].astype(BF16)

        @pl.when(t < root)
        def _():
            up_right(c).start()

        @pl.when(t > root)
        def _():
            up_left(c).start()

    def queue_part(c, _):
        p = (scores[zrows(c), :] * factor).astype(BF16)
        coef[zrows(c), :] = p
        part[zrows(c), :] = dot(p, clips[...])

        @pl.when(leaf)
        def _():
            send_up(c)

        return 0

    lax.fori_loop(0, ZC, queue_part, 0)

    def gather_up(c):
        @pl.when(left_child)
        def _():
            up_right(c).wait_recv()
            part[zrows(c), :] += up_rx[0, zrows(c), :].astype(F32)

        @pl.when(right_child)
        def _():
            up_left(c).wait_recv()
            part[zrows(c), :] += up_rx[1, zrows(c), :].astype(F32)

        @pl.when(t == root)
        def _():
            fin[zrows(c), :] = (scale * part[zrows(c), :]).astype(BF16)
            pass_down(c)

        @pl.when((t != root) & jnp.logical_not(leaf))
        def _():
            send_up(c)

    def take_down(c):
        @pl.when(t != root)
        def _():
            down_left(c).wait_recv()
            pass_down(c)

    def own_rows(index):
        return pl.ds(pl.multiple_of(index * own, own), own)

    def pair_copy(p):
        return remote(grad_b.at[own_rows(2 * p + 1 - core)], pair_rx.at[p],
                      pair_ss.at[p], pair_rs.at[p], (t, q + 1 - 2 * core))

    def pair_part(p, _):
        r = pl.ds(pl.multiple_of(p * 2 * own, 2 * own), 2 * own)
        g = dot(coef[:, r], queue[...], TN)
        grad_f[r, :] = g
        grad_b[r, :] = g.astype(BF16)
        pair_copy(p).start()
        return 0

    lax.fori_loop(0, chips, pair_part, 0)

    def chip_copy(k):
        peer = lax.rem(chip + k, chips)
        return remote(chip_tx.at[peer], chip_rx.at[k], chip_ss.at[k], chip_rs.at[k], (t, 2 * peer + core))

    def chip_part(k):
        p = lax.rem(chip + k, chips)
        pair_copy(p).wait_recv()
        g = grad_f[own_rows(2 * p + core), :] + pair_rx[p].astype(F32)
        if isinstance(k, int) and k == 0:
            grad_f[own_rows(2 * p + core), :] = g
        else:
            chip_tx[p] = g.astype(BF16)
            chip_copy(k).start()

    narr_acc[0:2 * PAD, :] = jnp.zeros((2 * PAD, width), F32)

    def narr_part(b):
        i0 = pl.multiple_of(b * BLK, BLK)
        c = bag_c[:, pl.ds(i0, BLK)]
        band = jnp.zeros((WIN, BLK), F32)
        for d in range(-HALO, HALO + 1):
            band = jnp.where(delta == d, c[d + HALO:d + HALO + 1, :], band)
        band = band.astype(BF16)
        g = dot(band, clips[pl.ds(i0, BLK), :])
        narr_acc[pl.ds(i0, 2 * PAD), :] += g[:2 * PAD]
        narr_acc[pl.ds(i0 + 2 * PAD, BLK), :] = g[2 * PAD:]

        @pl.when((i0 + BLK > q * own) & (i0 < (q + 1) * own))
        def _():
            bag_grad[pl.ds(i0, BLK), :] = dot(band, ext[pl.ds(i0, WIN), :], TN)

    chip_steps = -(-(chips - 1) // ZC)
    narr_steps = -(-blocks // ZC)

    def mixed(c, _):
        gather_up(c)
        for j in range(chip_steps):
            k = c * chip_steps + j + 1

            @pl.when(k < chips)
            def _():
                chip_part(k)

        for j in range(narr_steps):
            b = c * narr_steps + j

            @pl.when(b < blocks)
            def _():
                narr_part(b)

        @pl.when(c >= LAG)
        def _():
            take_down(c - LAG)

        return 0

    lax.fori_loop(0, ZC, mixed, 0)

    def edge_next():
        return remote(narr_acc.at[pl.ds(PAD + rows, PAD)], edge.at[0], edge_ss.at[0], edge_rs.at[0], (t + 1, q))

    def edge_prev():
        return remote(narr_acc.at[pl.ds(0, PAD)], edge.at[1], edge_ss.at[1], edge_rs.at[1], (t - 1, q))

    @pl.when(has_next)
    def _():
        edge_next().start()

    @pl.when(has_prev)
    def _():
        edge_prev().start()

    chip_part(0)
    g = grad_f[own_rows(q), :] + bag_grad[own_rows(q), :]
    for k in range(1, chips):
        chip_copy(k).wait_recv()
        g = g + chip_rx[k].astype(F32)
    gc_out[...] = (scale * g).astype(BF16)
    clips_store = pltpu.make_async_copy(gc_out, gc_hbm, out_sem.at[0])
    clips_store.start()

    @pl.when(has_prev)
    def _():
        edge_next().wait_recv()
        narr_acc[PAD:2 * PAD, :] += edge[0]

    @pl.when(has_next)
    def _():
        edge_prev().wait_recv()
        narr_acc[rows:rows + PAD, :] += edge[1]

    def narr_store(b, _):
        i0 = pl.multiple_of(b * BLK, BLK)
        gn_out[pl.ds(i0, BLK), :] = (scale * narr_acc[pl.ds(i0 + PAD, BLK), :]).astype(BF16)
        return 0

    lax.fori_loop(0, blocks, narr_store, 0)
    narr_out = pltpu.make_async_copy(gn_out, gn_hbm, out_sem.at[1])
    narr_out.start()

    for c in range(max(0, ZC - LAG), ZC):
        take_down(c)

    @pl.when(has_next)
    def _():
        halo_next().wait_send()
        edge_next().wait_send()

    @pl.when(has_prev)
    def _():
        halo_prev().wait_send()
        edge_prev().wait_send()

    for k in range(1, Q):
        stat_copy(k).wait_send()
    for k in range(chips):
        pair_copy(k).wait_send()
    for k in range(1, chips):
        chip_copy(k).wait_send()

    def drain(c, _):
        @pl.when(t < root)
        def _():
            up_right(c).wait_send()

        @pl.when(t > root)
        def _():
            up_left(c).wait_send()

        @pl.when(left_child)
        def _():
            down_left(c).wait_send()

        @pl.when(right_child)
        def _():
            down_right(c).wait_send()

        store_queue(c).wait()
        return 0

    lax.fori_loop(0, ZC, drain, 0)
    clips_store.wait()
    narr_out.wait()


def shards(T, Q, clips, narrations, queue, loss_weights, offsets, valid):
    rows, width = clips.shape
    negs = queue.shape[0]
    chips = Q // 2
    own = rows // Q
    zc = 8
    vmem = pl.BlockSpec(memory_space=pltpu.VMEM)
    hbm = pl.BlockSpec(memory_space=pl.ANY)
    dma = pltpu.SemaphoreType.DMA
    return pl.pallas_call(
        functools.partial(kernel, T, Q, zc),
        out_shape=(
            jax.ShapeDtypeStruct((own, width), BF16),
            jax.ShapeDtypeStruct((rows, width), BF16),
            jax.ShapeDtypeStruct((negs, width), BF16),
        ),
        in_specs=[vmem, hbm, vmem, vmem, vmem, vmem],
        out_specs=(hbm, hbm, hbm),
        scratch_shapes=[
            pltpu.VMEM((rows + 2 * PAD, width), BF16),
            pltpu.VMEM((negs, rows), F32),
            pltpu.VMEM((negs, rows), BF16),
            pltpu.VMEM((Q, 2, rows), F32),
            pltpu.VMEM((16, rows), F32),
            pltpu.VMEM((16, rows), F32),
            pltpu.VMEM((16, rows), F32),
            pltpu.VMEM((rows + 2 * PAD, width), F32),
            pltpu.VMEM((2, PAD, width), F32),
            pltpu.VMEM((negs, width), F32),
            pltpu.VMEM((negs, width), BF16),
            pltpu.VMEM((2, negs, width), BF16),
            pltpu.VMEM((negs, width), BF16),
            pltpu.VMEM((rows, width), F32),
            pltpu.VMEM((rows, width), BF16),
            pltpu.VMEM((chips, own, width), BF16),
            pltpu.VMEM((chips, own, width), BF16),
            pltpu.VMEM((chips, own, width), BF16),
            pltpu.VMEM((rows, width), F32),
            pltpu.VMEM((own, width), BF16),
            pltpu.VMEM((rows, width), BF16),
            dma, dma((2,)), dma((2,)), dma((Q,)), dma((Q,)),
            dma((zc,)), dma((2, zc)), dma((2, zc)), dma((zc,)),
            dma((chips,)), dma((chips,)), dma((chips,)), dma((chips,)),
            dma((2,)), dma((2,)), dma((zc,)), dma((2,)),
        ],
        compiler_params=pltpu.CompilerParams(
            collective_id=0, has_side_effects=True, vmem_limit_bytes=60 * 1024 * 1024),
        cost_estimate=pl.CostEstimate(
            flops=6 * rows * negs * width, bytes_accessed=8 * rows * width, transcendentals=rows * negs),
        name="mil_nce_grad",
    )(clips, narrations, queue, loss_weights[None, :], offsets.T, valid.T)


def solution(mesh):
    placed = (P("tm", None), P("tm", None), P("queue", None), P("tm"), P("tm", None), P("tm", None))
    return jax.shard_map(
        functools.partial(shards, mesh.shape["tm"], mesh.shape["queue"]),
        mesh=mesh,
        in_specs=placed,
        out_specs=(P(("tm", "queue"), None), P("tm", None), P("queue", None)),
        check_vma=False,
    )
```

```python
import functools
import math

import jax
import jax.numpy as jnp
from jax import lax
from jax.experimental import pallas as pl
from jax.experimental.pallas import tpu as pltpu
from jax.sharding import PartitionSpec as P

HALO = 4
PAD = 16
BLK = 128
WIN = BLK + 2 * PAD
LAG = 4
SUB = 2
MESH = pl.DeviceIdType.MESH
F32 = jnp.float32
BF16 = jnp.bfloat16
NT = (((1,), (1,)), ((), ()))
TN = (((0,), (0,)), ((), ()))


def dot(a, b, dims=(((1,), (0,)), ((), ()))):
    return lax.dot_general(a, b, dims, preferred_element_type=F32)


def kernel(T, Q, ZC, clips, narr_hbm, queue, weights, offsets, valid, gc_out, gn_out, fin,
           ext, scores, coef, stat, bag_s, counts, bag_c, narr_acc, edge, part, up_tx, up_rx,
           grad_f, grad_b, pair_rx, chip_tx, chip_rx, bag_grad,
           load_sem, halo_ss, halo_rs, stat_ss, stat_rs, up_ss, up_rs, down_ss, down_rs,
           pair_ss, pair_rs, chip_ss, chip_rs, edge_ss, edge_rs):
    rows, width = clips.shape
    negs = queue.shape[0]
    scale = 0.75 / math.sqrt(width)
    chips = Q // 2
    own = rows // Q
    zn = negs // ZC
    qn = zn * SUB
    steps = ZC // SUB
    blocks = rows // BLK
    root = (T - 1) // 2
    t = lax.axis_index("tm")
    q = lax.axis_index("queue")
    chip = q // 2
    core = lax.rem(q, 2)
    has_prev = t > 0
    has_next = t < T - 1

    def remote(src, dst, ss, rs, dev):
        return pltpu.make_async_remote_copy(
            src_ref=src, dst_ref=dst, send_sem=ss, recv_sem=rs, device_id=dev, device_id_type=MESH)

    barrier = pltpu.get_barrier_semaphore()
    for k in range(1, Q):
        pl.semaphore_signal(barrier, inc=1, device_id=(t, lax.rem(q + k, Q)), device_id_type=MESH)

    @pl.when(has_prev)
    def _():
        pl.semaphore_signal(barrier, inc=1, device_id=(t - 1, q), device_id_type=MESH)

    @pl.when(has_next)
    def _():
        pl.semaphore_signal(barrier, inc=1, device_id=(t + 1, q), device_id_type=MESH)

    load = pltpu.make_async_copy(narr_hbm, ext.at[pl.ds(PAD, rows)], load_sem)
    load.start()

    SN = 256

    def score_step(k, top):
        r = pl.ds(pl.multiple_of(k * SN, SN), SN)
        s = scale * dot(queue[r, :], clips[...], NT)
        scores[r, :] = s
        return jnp.maximum(top, jnp.max(s, axis=0, keepdims=True))

    top = lax.fori_loop(0, negs // SN, score_step, jnp.full((1, rows), -jnp.inf, F32))

    load.wait()
    pl.semaphore_wait(barrier, Q - 1 + has_prev.astype(jnp.int32) + has_next.astype(jnp.int32))

    def halo_next():
        return remote(ext.at[pl.ds(rows, PAD)], ext.at[pl.ds(0, PAD)],
                      halo_ss.at[0], halo_rs.at[0], (t + 1, q))

    def halo_prev():
        return remote(ext.at[pl.ds(PAD, PAD)], ext.at[pl.ds(PAD + rows, PAD)],
                      halo_ss.at[1], halo_rs.at[1], (t - 1, q))

    @pl.when(has_next)
    def _():
        halo_next().start()

    @pl.when(has_prev)
    def _():
        halo_prev().start()

    EN = 32

    def exp_step(k, total):
        r = pl.ds(pl.multiple_of(k * EN, EN), EN)
        p = jnp.exp(scores[r, :] - top)
        scores[r, :] = p
        return total + jnp.sum(p, axis=0, keepdims=True)

    local_sum = lax.fori_loop(0, negs // EN, exp_step, jnp.zeros((1, rows), F32))
    stat[q, 0:1, :] = top
    stat[q, 1:2, :] = local_sum

    def stat_copy(k):
        peer = lax.rem(q + k, Q)
        return remote(stat.at[q], stat.at[q], stat_ss.at[k], stat_rs.at[k], (t, peer))

    def stat_arrival(k):
        source = lax.rem(q + Q - k, Q)
        return remote(stat.at[source], stat.at[source], stat_ss.at[k], stat_rs.at[k], (t, source))

    for k in range(1, Q):
        stat_copy(k).start()

    @pl.when(has_prev)
    def _():
        halo_next().wait_recv()

    @pl.when(jnp.logical_not(has_prev))
    def _():
        ext[0:PAD, :] = jnp.zeros((PAD, width), BF16)

    @pl.when(has_next)
    def _():
        halo_prev().wait_recv()

    @pl.when(jnp.logical_not(has_next))
    def _():
        ext[PAD + rows:, :] = jnp.zeros((PAD, width), BF16)

    bag_s[...] = jnp.zeros_like(bag_s)
    counts[...] = jnp.zeros_like(counts)
    delta = (lax.broadcasted_iota(jnp.int32, (WIN, BLK), 0)
             - lax.broadcasted_iota(jnp.int32, (WIN, BLK), 1) - PAD)

    def bag_step(b, _):
        i0 = pl.multiple_of(b * BLK, BLK)
        s = scale * dot(ext[pl.ds(i0, WIN), :], clips[pl.ds(i0, BLK), :], NT)
        for d in range(-HALO, HALO + 1):
            bag_s[d + HALO:d + HALO + 1, pl.ds(i0, BLK)] = jnp.sum(
                jnp.where(delta == d, s, 0.0), axis=0, keepdims=True)
        return 0

    lax.fori_loop(0, blocks, bag_step, 0)

    position = t * rows + lax.broadcasted_iota(jnp.int32, (1, rows), 1)
    used = valid[...] > 0
    for d in range(-HALO, HALO + 1):
        hits = jnp.sum(jnp.where(used & (offsets[...] == d), 1.0, 0.0), axis=0, keepdims=True)
        inside = (position + d >= 0) & (position + d < T * rows)
        counts[d + HALO:d + HALO + 1, :] = jnp.where(inside, hits + (1.0 if d == 0 else 0.0), 0.0)
    count = counts[...]
    bag_top = jnp.max(jnp.where(count > 0, bag_s[...], -jnp.inf), axis=0, keepdims=True)
    bag_e = jnp.where(count > 0, count * jnp.exp(bag_s[...] - bag_top), 0.0)
    bag_sum = jnp.sum(bag_e, axis=0, keepdims=True)

    for k in range(1, Q):
        stat_arrival(k).wait_recv()
    shift = bag_top
    for k in range(Q):
        shift = jnp.maximum(shift, stat[k, 0:1, :])
    bag_part = bag_sum * jnp.exp(bag_top - shift)
    total = bag_part
    for k in range(Q):
        total = total + stat[k, 1:2, :] * jnp.exp(stat[k, 0:1, :] - shift)
    share = bag_part / total
    w = weights[...]
    factor = w / total * jnp.exp(top - shift)
    bag_c[...] = (w * bag_e / bag_sum * (share - 1.0)).astype(BF16).astype(F32)

    left_child = has_prev & (t <= root)
    right_child = has_next & (t >= root)
    leaf = jnp.logical_not(left_child | right_child)

    def zrows(c):
        return pl.ds(pl.multiple_of(c * zn, zn), zn)

    def up_right(c):
        return remote(up_tx.at[zrows(c)], up_rx.at[0, zrows(c)], up_ss.at[c], up_rs.at[0, c], (t + 1, q))

    def up_left(c):
        return remote(up_tx.at[zrows(c)], up_rx.at[1, zrows(c)], up_ss.at[c], up_rs.at[1, c], (t - 1, q))

    def down_left(c):
        return remote(fin.at[zrows(c)], fin.at[zrows(c)], down_ss.at[0, c], down_rs.at[c], (t - 1, q))

    def down_right(c):
        return remote(fin.at[zrows(c)], fin.at[zrows(c)], down_ss.at[1, c], down_rs.at[c], (t + 1, q))

    def pass_down(c):
        @pl.when(left_child)
        def _():
            down_left(c).start()

        @pl.when(right_child)
        def _():
            down_right(c).start()

    def send_up(c):
        up_tx[zrows(c), :] = part[zrows(c), :].astype(BF16)

        @pl.when(t < root)
        def _():
            up_right(c).start()

        @pl.when(t > root)
        def _():
            up_left(c).start()

    def queue_part(c, _):
        r = pl.ds(pl.multiple_of(c * qn, qn), qn)
        p = (scores[r, :] * factor).astype(BF16)
        coef[r, :] = p
        part[r, :] = dot(p, clips[...])

        @pl.when(leaf)
        def _():
            for j in range(SUB):
                send_up(c * SUB + j)

        return 0

    def gather_up(c):
        @pl.when(left_child)
        def _():
            up_right(c).wait_recv()
            part[zrows(c), :] += up_rx[0, zrows(c), :].astype(F32)

        @pl.when(right_child)
        def _():
            up_left(c).wait_recv()
            part[zrows(c), :] += up_rx[1, zrows(c), :].astype(F32)

        @pl.when(t == root)
        def _():
            fin[zrows(c), :] = (scale * part[zrows(c), :]).astype(BF16)
            pass_down(c)

        @pl.when((t != root) & jnp.logical_not(leaf))
        def _():
            send_up(c)

    def take_down(c):
        @pl.when(t != root)
        def _():
            down_left(c).wait_recv()
            pass_down(c)

    def own_rows(index):
        return pl.ds(pl.multiple_of(index * own, own), own)

    def pair_copy(p):
        return remote(grad_b.at[own_rows(2 * p + 1 - core)], pair_rx.at[p],
                      pair_ss.at[p], pair_rs.at[p], (t, q + 1 - 2 * core))

    def pair_part(p):
        r = pl.ds(pl.multiple_of(p * 2 * own, 2 * own), 2 * own)
        g = dot(coef[:, r], queue[...], TN)
        grad_f[r, :] = g
        grad_b[r, :] = g.astype(BF16)
        pair_copy(p).start()

    def chip_copy(k):
        peer = lax.rem(chip + k, chips)
        return remote(chip_tx.at[peer], chip_rx.at[k], chip_ss.at[k], chip_rs.at[k], (t, 2 * peer + core))

    def chip_part(k):
        p = lax.rem(chip + k, chips)
        pair_copy(p).wait_recv()
        g = grad_f[own_rows(2 * p + core), :] + pair_rx[p].astype(F32)
        if isinstance(k, int) and k == 0:
            grad_f[own_rows(2 * p + core), :] = g
        else:
            chip_tx[p] = g.astype(BF16)
            chip_copy(k).start()

    narr_acc[0:2 * PAD, :] = jnp.zeros((2 * PAD, width), F32)

    def narr_part(b):
        i0 = pl.multiple_of(b * BLK, BLK)
        c = bag_c[:, pl.ds(i0, BLK)]
        band = jnp.zeros((WIN, BLK), F32)
        for d in range(-HALO, HALO + 1):
            band = jnp.where(delta == d, c[d + HALO:d + HALO + 1, :], band)
        band = band.astype(BF16)
        g = dot(band, clips[pl.ds(i0, BLK), :])
        narr_acc[pl.ds(i0, 2 * PAD), :] += g[:2 * PAD]
        narr_acc[pl.ds(i0 + 2 * PAD, BLK), :] = g[2 * PAD:]

        @pl.when((i0 + BLK > q * own) & (i0 < (q + 1) * own))
        def _():
            bag_grad[pl.ds(i0, BLK), :] = dot(band, ext[pl.ds(i0, WIN), :], TN)

    middle = (left_child | right_child) & (t != root)
    chip_from = ZC // 4 + 1
    pair_steps = -(-chips // (ZC // 4))
    chip_steps = -(-(chips - 1) // (ZC - chip_from))
    narr_steps = -(-blocks // ZC)

    def guarded(index, start, stop, work):
        @pl.when((index >= start) & (index < stop))
        def _():
            work(index)

    def mixed(c, _):
        gather_up(c)

        @pl.when(middle & (c >= LAG))
        def _():
            take_down(c - LAG)

        for j in range(pair_steps):
            guarded(c * pair_steps + j, 0, chips, pair_part)
        for j in range(chip_steps):
            guarded((c - chip_from) * chip_steps + j + 1, 1, chips, chip_part)
        for j in range(narr_steps):
            guarded(c * narr_steps + j, 0, blocks, narr_part)
        return 0

    lax.fori_loop(0, steps, queue_part, 0)
    lax.fori_loop(0, ZC, mixed, 0)

    def edge_next():
        return remote(narr_acc.at[pl.ds(PAD + rows, PAD)], edge.at[0], edge_ss.at[0], edge_rs.at[0], (t + 1, q))

    def edge_prev():
        return remote(narr_acc.at[pl.ds(0, PAD)], edge.at[1], edge_ss.at[1], edge_rs.at[1], (t - 1, q))

    @pl.when(has_next)
    def _():
        edge_next().start()

    @pl.when(has_prev)
    def _():
        edge_prev().start()

    chip_part(0)
    g = grad_f[own_rows(q), :] + bag_grad[own_rows(q), :]
    for k in range(1, chips):
        chip_copy(k).wait_recv()
        g = g + chip_rx[k].astype(F32)
    gc_out[...] = (scale * g).astype(BF16)

    @pl.when(has_prev)
    def _():
        edge_next().wait_recv()
        narr_acc[PAD:2 * PAD, :] += edge[0]

    @pl.when(has_next)
    def _():
        edge_prev().wait_recv()
        narr_acc[rows:rows + PAD, :] += edge[1]

    def narr_store(b, _):
        i0 = pl.multiple_of(b * BLK, BLK)
        gn_out[pl.ds(i0, BLK), :] = (scale * narr_acc[pl.ds(i0 + PAD, BLK), :]).astype(BF16)
        return 0

    lax.fori_loop(0, blocks, narr_store, 0)

    for c in range(max(0, ZC - LAG), ZC):
        @pl.when(middle)
        def _():
            take_down(c)

    def last_down(c, _):
        take_down(c)
        return 0

    @pl.when(leaf)
    def _():
        lax.fori_loop(0, ZC, last_down, 0)

    @pl.when(has_next)
    def _():
        halo_next().wait_send()
        edge_next().wait_send()

    @pl.when(has_prev)
    def _():
        halo_prev().wait_send()
        edge_prev().wait_send()

    for k in range(1, Q):
        stat_copy(k).wait_send()
    for k in range(chips):
        pair_copy(k).wait_send()
    for k in range(1, chips):
        chip_copy(k).wait_send()

    def drain(c, _):
        @pl.when(t < root)
        def _():
            up_right(c).wait_send()

        @pl.when(t > root)
        def _():
            up_left(c).wait_send()

        @pl.when(left_child)
        def _():
            down_left(c).wait_send()

        @pl.when(right_child)
        def _():
            down_right(c).wait_send()

        return 0

    lax.fori_loop(0, ZC, drain, 0)


def store_kernel(*refs):
    sources, targets, sem = refs[:3], refs[3:6], refs[6]
    copies = [pltpu.make_async_copy(sources[k], targets[k], sem.at[k]) for k in range(3)]
    for copy in copies:
        copy.start()
    for copy in copies:
        copy.wait()


def shards(T, Q, clips, narrations, queue, loss_weights, offsets, valid):
    rows, width = clips.shape
    negs = queue.shape[0]
    chips = Q // 2
    own = rows // Q
    zc = 16
    vmem = pl.BlockSpec(memory_space=pltpu.VMEM)
    hbm = pl.BlockSpec(memory_space=pl.ANY)
    dma = pltpu.SemaphoreType.DMA
    grads = pl.pallas_call(
        functools.partial(kernel, T, Q, zc),
        out_shape=(
            pltpu.VMEM((own, width), BF16),
            pltpu.VMEM((rows, width), BF16),
            pltpu.VMEM((negs, width), BF16),
        ),
        in_specs=[vmem, hbm, vmem, vmem, vmem, vmem],
        out_specs=(vmem, vmem, vmem),
        scratch_shapes=[
            pltpu.VMEM((rows + 2 * PAD, width), BF16),
            pltpu.VMEM((negs, rows), F32),
            pltpu.VMEM((negs, rows), BF16),
            pltpu.VMEM((Q, 2, rows), F32),
            pltpu.VMEM((16, rows), F32),
            pltpu.VMEM((16, rows), F32),
            pltpu.VMEM((16, rows), F32),
            pltpu.VMEM((rows + 2 * PAD, width), F32),
            pltpu.VMEM((2, PAD, width), F32),
            pltpu.VMEM((negs, width), F32),
            pltpu.VMEM((negs, width), BF16),
            pltpu.VMEM((2, negs, width), BF16),
            pltpu.VMEM((rows, width), F32),
            pltpu.VMEM((rows, width), BF16),
            pltpu.VMEM((chips, own, width), BF16),
            pltpu.VMEM((chips, own, width), BF16),
            pltpu.VMEM((chips, own, width), BF16),
            pltpu.VMEM((rows, width), F32),
            dma, dma((2,)), dma((2,)), dma((Q,)), dma((Q,)),
            dma((zc,)), dma((2, zc)), dma((2, zc)), dma((zc,)),
            dma((chips,)), dma((chips,)), dma((chips,)), dma((chips,)),
            dma((2,)), dma((2,)),
        ],
        compiler_params=pltpu.CompilerParams(
            collective_id=0, has_side_effects=True, vmem_limit_bytes=52 * 1024 * 1024),
        cost_estimate=pl.CostEstimate(
            flops=6 * rows * negs * width, bytes_accessed=8 * rows * width, transcendentals=rows * negs),
        name="mil_nce_grad",
    )(clips, narrations, queue, loss_weights[None, :], offsets.T, valid.T)
    return pl.pallas_call(
        store_kernel,
        out_shape=tuple(jax.ShapeDtypeStruct(g.shape, g.dtype) for g in grads),
        in_specs=[vmem] * 3,
        out_specs=(hbm,) * 3,
        scratch_shapes=[dma((3,))],
        name="store_grads",
    )(*[pltpu.with_memory_space_constraint(g, pltpu.VMEM) for g in grads])


def solution(mesh):
    placed = (P("tm", None), P("tm", None), P("queue", None), P("tm"), P("tm", None), P("tm", None))
    return jax.shard_map(
        functools.partial(shards, mesh.shape["tm"], mesh.shape["queue"]),
        mesh=mesh,
        in_specs=placed,
        out_specs=(P(("tm", "queue"), None), P("tm", None), P("queue", None)),
        check_vma=False,
    )
```
